32 devices in a mesh: row: 8 (over z, y), col: 4 (over x, core).
Axes of the slice: x: 2, y: 2, z: 4, core: 2. Of those that a mesh axis runs over, the one named last changes fastest.
Arguments:
- tokens: bfloat16 [512, 12288], P('col', 'row'), may hold values from -6 to 6
- in_weight: bfloat16 [12288, 24576], P('row', 'col'), may hold values from -0.0546875 to 0.0546875
- out_weight: bfloat16 [24576, 12288], P('col', 'row'), may hold values from -0.0390625 to 0.0390625
- out_grad: bfloat16 [512, 12288], P('col', 'row'), may hold values from -6 to 6
Outputs:
- layer_out: bfloat16 [512, 12288], P('col', 'row')
- token_grad: bfloat16 [512, 12288], P('col', 'row')
- first_grad: bfloat16 [12288, 24576], P('row', 'col')
- second_grad: bfloat16 [24576, 12288], P('col', 'row')
The draws below stay inside these ranges and needn't reach their ends.
All inputs are finite; a program needn't handle non-finite values.
Results may differ from the reference program's by a relative error of at most 0.005.
Values may be sent and summed in bfloat16 or wider, within the bound.
A program may use at most 192 MiB of HBM per device.

```python
import jax
import jax.numpy as jnp
from jax import lax

D = 12288
FF = 24576
TOKENS = 512


def steps_of(rng, extent, pieces, low, largest):
    gain = 1.0
    for dim, parts in pieces:
        heights = jax.random.uniform(jax.random.fold_in(jax.random.fold_in(rng, 6), dim), (parts,), jnp.float32, low / len(pieces), largest / len(pieces))
        gain = gain * jnp.repeat(jnp.exp(heights), extent[dim] // parts).reshape((-1,) + (1,) * (len(extent) - 1 - dim))
    return gain


def gaussian(rng, shape, spread, bound, cuts=(), kind=jnp.bfloat16):
    values = spread * jax.random.normal(rng, shape, jnp.float32)
    if cuts:
        values = values * steps_of(rng, shape, cuts, -0.22, 0.18)
    return jnp.clip(values, -bound, bound).astype(kind)


def setup_inputs(seed: int = 0) -> dict:
    arg_keys = jax.random.split(jax.random.key(seed), 5)
    tokens = gaussian(arg_keys[0], (TOKENS, D), 1.0, 6.0, ((0, 4), (1, 8)))
    in_weight = gaussian(arg_keys[1], (D, FF), D ** -0.5, 0.0546875, ((0, 8), (1, 4)))
    out_weight = gaussian(arg_keys[2], (FF, D), FF ** -0.5, 0.0390625, ((0, 4), (1, 8)))
    out_grad = gaussian(arg_keys[3], (TOKENS, D), 1.0, 6.0, ((0, 4), (1, 8)))
    return dict(tokens=tokens, in_weight=in_weight, out_weight=out_weight, out_grad=out_grad)


gelu_c = 0.7978845608
gelu_k = 0.044715


def gelu_value(pre):
    inner = jnp.tanh(gelu_c * (pre + gelu_k * pre * pre * pre))
    return 0.5 * pre * (1.0 + inner)


def gelu_slope(pre):
    inner = jnp.tanh(gelu_c * (pre + gelu_k * pre * pre * pre))
    return 0.5 * (1.0 + inner) + 0.5 * pre * (1.0 - inner * inner) * gelu_c * (1.0 + 3.0 * gelu_k * pre * pre)


def reference(tokens, in_weight, out_weight, out_grad):
    pre = jnp.dot(tokens, in_weight, preferred_element_type=jnp.float32)
    hidden = gelu_value(pre).astype(jnp.bfloat16)
    layer_out = jnp.dot(hidden, out_weight, preferred_element_type=jnp.float32).astype(jnp.bfloat16)
    hidden_grad = lax.dot_general(out_grad, out_weight, (((1,), (1,)), ((), ())), preferred_element_type=jnp.float32)
    pre_grad = (hidden_grad * gelu_slope(pre)).astype(jnp.bfloat16)
    first_grad = lax.dot_general(tokens, pre_grad, (((0,), (0,)), ((), ())), preferred_element_type=jnp.float32).astype(jnp.bfloat16)
    second_grad = lax.dot_general(hidden, out_grad, (((0,), (0,)), ((), ())), preferred_element_type=jnp.float32).astype(jnp.bfloat16)
    token_grad = lax.dot_general(pre_grad, in_weight, (((1,), (1,)), ((), ())), preferred_element_type=jnp.float32).astype(jnp.bfloat16)
    return layer_out, token_grad, first_grad, second_grad
```

```python
import functools

import jax
import jax.numpy as jnp
from jax import lax
from jax.experimental import pallas as pl
from jax.experimental.pallas import tpu as pltpu
from jax.sharding import PartitionSpec as P

gelu_c = 0.7978845608
gelu_k = 0.044715
f32, bf16 = jnp.float32, jnp.bfloat16
LAG = 2


def dot_last(left, right):
    return lax.dot_general(left, right, (((1,), (1,)), ((), ())), preferred_element_type=f32)


def dot_first(left, right):
    return lax.dot_general(left, right, (((0,), (0,)), ((), ())), preferred_element_type=f32)


def kernel(
    nz, ncol, chunks, width,
    tok, grad, w1, w2,
    out, lo, tg, tall, gall,
    part, yr, zr, w1a, w2a, w1b, w2b,
    wsem_a, wsem_b, gs, gr, ys, yrs, zs, zrs, azs, azr, ays, ayr,
):
    row, col = lax.axis_index("row"), lax.axis_index("col")
    z, y = row // 2, row % 2
    share, total = tok.shape[0], tall.shape[0]
    half = total // 2
    blk = half // nz
    rows_step = min(256, total)

    y_peer = {"row": z * 2 + (1 - y)}
    z_at = [lax.rem(z + d, nz) for d in range(1, nz)]
    z_peers = [{"row": p * 2 + y} for p in z_at]
    c_peers = [{"col": lax.rem(col + d, ncol)} for d in range(1, ncol)]

    def cols(c):
        return pl.ds(pl.multiple_of(c * width, width), width)

    def fetch(c, b1, b2, sem):
        slot = lax.rem(c, 2)
        return (
            pltpu.make_async_copy(w1.at[:, cols(c)], b1.at[slot], sem.at[slot, 0]),
            pltpu.make_async_copy(w2.at[cols(c), :], b2.at[slot], sem.at[slot, 1]),
        )

    for copy in fetch(0, w1a, w2a, wsem_a) + fetch(0, w1b, w2b, wsem_b):
        copy.start()

    barrier = pltpu.get_barrier_semaphore()
    peers = [y_peer] + z_peers + c_peers
    for peer in peers:
        pl.semaphore_signal(barrier, inc=1, device_id=peer, device_id_type=pl.DeviceIdType.MESH)
    pl.semaphore_wait(barrier, len(peers))

    def send(src, dst, s_sem, r_sem, peer):
        pltpu.make_async_remote_copy(
            src_ref=src, dst_ref=dst, send_sem=s_sem, recv_sem=r_sem,
            device_id=peer, device_id_type=pl.DeviceIdType.MESH,
        ).start()

    def drain(like, sem):
        pltpu.make_async_copy(like, like, sem).wait()

    mine = pl.ds(pl.multiple_of(col * share, share), share)
    for peer in c_peers:
        send(tok, tall.at[mine], gs.at[0], gr.at[0], peer)
        send(grad, gall.at[mine], gs.at[1], gr.at[1], peer)
    tall[mine] = tok[...]
    gall[mine] = grad[...]
    lo[...] = jnp.zeros_like(lo)
    tg[...] = jnp.zeros_like(tg)
    rest = pl.ds(0, (ncol - 1) * share)
    drain(tall.at[rest], gr.at[0])
    drain(gall.at[rest], gr.at[1])
    drain(tall.at[rest], gs.at[0])
    drain(gall.at[rest], gs.at[1])

    own_half = pl.ds(pl.multiple_of(y * half, half), half)
    other_half = pl.ds(pl.multiple_of((1 - y) * half, half), half)

    def block(p):
        return pl.ds(pl.multiple_of(y * half + p * blk, blk), blk)

    def front(c):
        slot = lax.rem(c, 2)

        @pl.when(c + 1 < chunks)
        def _():
            for copy in fetch(c + 1, w1a, w2a, wsem_a):
                copy.start()

        for copy in fetch(c, w1a, w2a, wsem_a):
            copy.wait()

        @pl.loop(0, total // rows_step)
        def _(i):
            r = pl.ds(pl.multiple_of(i * rows_step, rows_step), rows_step)
            part[0, r, cols(c)] = jnp.dot(
                tall[r, :], w1a[slot], preferred_element_type=f32
            ).astype(bf16)
            part[1, r, cols(c)] = dot_last(gall[r, :], w2a[slot]).astype(bf16)

        send(part.at[:, other_half, cols(c)], yr.at[:, :, cols(c)], ys.at[c], yrs.at[c], y_peer)

    def sum_y(c):
        drain(yr.at[:, :, cols(c)], yrs.at[c])
        drain(yr.at[:, :, cols(c)], ys.at[c])
        part[:, own_half, cols(c)] = (
            part[:, own_half, cols(c)].astype(f32) + yr[:, :, cols(c)].astype(f32)
        ).astype(bf16)
        for d, peer in enumerate(z_peers):
            send(
                part.at[:, block(z_at[d]), cols(c)], zr.at[d, :, :, cols(c)],
                zs.at[c], zrs.at[c], peer,
            )

    def sum_z(c):
        drain(zr.at[:, :, :, cols(c)], zrs.at[c])
        drain(zr.at[:, :, :, cols(c)], zs.at[c])
        both = part[:, block(z), cols(c)].astype(f32)
        for d in range(nz - 1):
            both = both + zr[d, :, :, cols(c)].astype(f32)
        pre, hid = both[0], both[1]
        t = jnp.tanh(gelu_c * (pre + gelu_k * pre * pre * pre))
        slope = 0.5 * (1.0 + t) + 0.5 * pre * (1.0 - t * t) * gelu_c * (
            1.0 + 3.0 * gelu_k * pre * pre
        )
        out[0, block(z), cols(c)] = (0.5 * pre * (1.0 + t)).astype(bf16)
        out[1, block(z), cols(c)] = (hid * slope).astype(bf16)
        at = out.at[:, block(z), cols(c)]
        for peer in z_peers:
            send(at, at, azs.at[c], azr.at[c], peer)

    def give_y(c):
        drain(zr.at[:, :, :, cols(c)], azr.at[c])
        drain(zr.at[:, :, :, cols(c)], azs.at[c])
        at = out.at[:, own_half, cols(c)]
        send(at, at, ays.at[c], ayr.at[c], y_peer)

    def back(c):
        slot = lax.rem(c, 2)

        @pl.when(c + 1 < chunks)
        def _():
            for copy in fetch(c + 1, w1b, w2b, wsem_b):
                copy.start()

        for copy in fetch(c, w1b, w2b, wsem_b):
            copy.wait()
        drain(yr.at[:, :, cols(c)], ayr.at[c])
        drain(yr.at[:, :, cols(c)], ays.at[c])

        @pl.loop(0, total // rows_step)
        def _(i):
            r = pl.ds(pl.multiple_of(i * rows_step, rows_step), rows_step)
            lo[r, :] += jnp.dot(out[0, r, cols(c)], w2b[slot], preferred_element_type=f32)
            tg[r, :] += dot_last(out[1, r, cols(c)], w1b[slot])

    stages = (front, sum_y, sum_z, give_y, back)

    @pl.loop(0, chunks + LAG * (len(stages) - 1))
    def _(s):
        for n, stage in enumerate(stages):
            c = s - n * LAG

            @pl.when(jnp.logical_and(c >= 0, c < chunks))
            def _(stage=stage, c=c):
                stage(c)


def per_device(nrow, ncol, tokens, in_weight, out_weight, out_grad):
    nz = nrow // 2
    share, feats = tokens.shape
    total = share * ncol
    hid = in_weight.shape[1]
    width = 256
    chunks = hid // width
    half, blk = total // 2, total // nrow
    vmem = pl.BlockSpec(memory_space=pltpu.VMEM)
    hbm = pl.BlockSpec(memory_space=pl.ANY)
    dma = pltpu.SemaphoreType.DMA
    both, lo, tg, all_tokens, all_grads = pl.pallas_call(
        functools.partial(kernel, nz, ncol, chunks, width),
        out_shape=(
            jax.ShapeDtypeStruct((2, total, hid), bf16),
            jax.ShapeDtypeStruct((total, feats), f32),
            jax.ShapeDtypeStruct((total, feats), f32),
            jax.ShapeDtypeStruct((total, feats), bf16),
            jax.ShapeDtypeStruct((total, feats), bf16),
        ),
        in_specs=[vmem, vmem, hbm, hbm],
        out_specs=(vmem,) * 5,
        scratch_shapes=[
            pltpu.VMEM((2, total, hid), bf16),
            pltpu.VMEM((2, half, hid), bf16),
            pltpu.VMEM((nz - 1, 2, blk, hid), bf16),
            pltpu.VMEM((2, feats, width), bf16),
            pltpu.VMEM((2, width, feats), bf16),
            pltpu.VMEM((2, feats, width), bf16),
            pltpu.VMEM((2, width, feats), bf16),
            dma((2, 2)),
            dma((2, 2)),
            dma((2,)),
            dma((2,)),
        ]
        + [dma((chunks,))] * 8,
        compiler_params=pltpu.CompilerParams(
            collective_id=0, has_side_effects=True, vmem_limit_bytes=62 * 1024 * 1024
        ),
        cost_estimate=pl.CostEstimate(
            flops=8 * total * feats * hid,
            bytes_accessed=8 * feats * hid + 4 * total * hid,
            transcendentals=blk * hid,
        ),
    )(tokens, out_grad, in_weight, out_weight)
    layer_out = lax.psum_scatter(lo, "col", scatter_dimension=0, tiled=True).astype(bf16)
    token_grad = lax.psum_scatter(tg, "col", scatter_dimension=0, tiled=True).astype(bf16)
    second_grad = dot_first(both[0], all_grads).astype(bf16)
    first_grad = dot_first(all_tokens, both[1]).astype(bf16)
    return (layer_out, token_grad, first_grad, second_grad)


def solution(mesh):
    return jax.shard_map(
        functools.partial(per_device, mesh.shape["row"], mesh.shape["col"]),
        mesh=mesh,
        in_specs=(P("col", "row"), P("row", "col"), P("col", "row"), P("col", "row")),
        out_specs=(P("col", "row"), P("col", "row"), P("row", "col"), P("col", "row")),
        check_vma=False,
    )
```

```python
import functools

import jax
import jax.numpy as jnp
from jax import lax
from jax.experimental import pallas as pl
from jax.experimental.pallas import tpu as pltpu
from jax.sharding import PartitionSpec as P

gelu_c = 0.7978845608
gelu_k = 0.044715
f32, bf16 = jnp.float32, jnp.bfloat16
LAG = 2


def dot_last(left, right):
    return lax.dot_general(left, right, (((1,), (1,)), ((), ())), preferred_element_type=f32)


def dot_first(left, right):
    return lax.dot_general(left, right, (((0,), (0,)), ((), ())), preferred_element_type=f32)


def kernel(
    nz, ncol, chunks, width,
    tok, grad, w1, w2,
    out, ends, tall, gall,
    part, mid, own, acc, yr, zr, w1a, w2a, w1b, w2b,
    wsem_a, wsem_b, gs, gr, ys, yrs, zs, zrs, azs, azr, ays, ayr,
):
    row, col = lax.axis_index("row"), lax.axis_index("col")
    z, y = row // 2, row % 2
    share, total = tok.shape[0], tall.shape[0]
    half = total // 2
    blk = half // nz
    rows_step = min(256, half)
    feats = tok.shape[1]
    keep = own.shape[0]
    group, core = col // 2, col % 2
    groups = ncol // 2

    y_peer = {"row": z * 2 + (1 - y)}
    z_at = [lax.rem(z + d, nz) for d in range(1, nz)]
    z_peers = [{"row": p * 2 + y} for p in z_at]
    c_at = [lax.rem(group + d, groups) * 2 + core for d in range(1, groups)]
    c_peers = [{"col": p} for p in c_at]
    twin = {"col": group * 2 + (1 - core)}

    def cols(c):
        return pl.ds(pl.multiple_of(c * width, width), width)

    def fetch(c, b1, b2, sem):
        slot = lax.rem(c, 2)
        return (
            pltpu.make_async_copy(w1.at[:, cols(c)], b1.at[slot], sem.at[slot, 0]),
            pltpu.make_async_copy(w2.at[cols(c), :], b2.at[slot], sem.at[slot, 1]),
        )

    for copy in fetch(0, w1a, w2a, wsem_a) + fetch(0, w1b, w2b, wsem_b):
        copy.start()

    barrier = pltpu.get_barrier_semaphore()
    peers = [y_peer, twin] + z_peers + c_peers
    for peer in peers:
        pl.semaphore_signal(barrier, inc=1, device_id=peer, device_id_type=pl.DeviceIdType.MESH)
    pl.semaphore_wait(barrier, len(peers))

    def send(src, dst, s_sem, r_sem, peer):
        pltpu.make_async_remote_copy(
            src_ref=src, dst_ref=dst, send_sem=s_sem, recv_sem=r_sem,
            device_id=peer, device_id_type=pl.DeviceIdType.MESH,
        ).start()

    def drain(like, sem):
        pltpu.make_async_copy(like, like, sem).wait()

    def place(p):
        return pl.ds(pl.multiple_of(p * share, share), share)

    gathers = ((tok, tall), (grad, gall))
    for n, (src, dst) in enumerate(gathers):
        for peer in c_peers:
            send(src, dst.at[place(col)], gs.at[n, 0], gr.at[n, 0], peer)
    for n, (src, dst) in enumerate(gathers):
        send(src, dst.at[place(col)], gs.at[n, 1], gr.at[n, 1], twin)
    tall[place(col)] = tok[...]
    gall[place(col)] = grad[...]
    acc[...] = jnp.zeros_like(acc)
    rest, one = pl.ds(0, (groups - 1) * share), pl.ds(0, share)
    for n, (src, dst) in enumerate(gathers):
        drain(dst.at[rest], gr.at[n, 0])
        for p in c_at:
            send(dst.at[place(p)], dst.at[place(p)], gs.at[n, 2], gr.at[n, 2], twin)
    for n, (src, dst) in enumerate(gathers):
        drain(dst.at[rest], gs.at[n, 0])
        drain(dst.at[one], gs.at[n, 1])
        drain(dst.at[one], gr.at[n, 1])
        drain(dst.at[rest], gs.at[n, 2])
        drain(dst.at[rest], gr.at[n, 2])

    own_half = pl.ds(pl.multiple_of(y * half, half), half)

    def block(p):
        return pl.ds(pl.multiple_of(y * half + p * blk, blk), blk)

    def front(c):
        slot = lax.rem(c, 2)

        @pl.when(c + 1 < chunks)
        def _():
            for copy in fetch(c + 1, w1a, w2a, wsem_a):
                copy.start()

        for copy in fetch(c, w1a, w2a, wsem_a):
            copy.wait()

        def rows(base, i):
            return pl.ds(pl.multiple_of(base * half + i * rows_step, rows_step), rows_step)

        @pl.loop(0, half // rows_step)
        def _(i):
            r, to = rows(1 - y, i), rows(0, i)
            part[0, to, cols(c)] = jnp.dot(
                tall[r, :], w1a[slot], preferred_element_type=f32
            ).astype(bf16)
            part[1, to, cols(c)] = dot_last(gall[r, :], w2a[slot]).astype(bf16)

        at = yr.at[:, :, cols(c)]
        send(part.at[:, :, cols(c)], at, ys.at[c], yrs.at[c], y_peer)
        mine = lax.rem(c, keep)

        @pl.loop(0, half // rows_step)
        def _(i):
            r, to = rows(y, i), rows(0, i)
            own[mine, 0, to, :] = jnp.dot(tall[r, :], w1a[slot], preferred_element_type=f32)
            own[mine, 1, to, :] = dot_last(gall[r, :], w2a[slot])

    def sum_y(c):
        drain(yr.at[:, :, cols(c)], yrs.at[c])
        drain(yr.at[:, :, cols(c)], ys.at[c])
        mine = lax.rem(c, keep)
        total_y = own[mine] + yr[:, :, cols(c)].astype(f32)
        own[mine] = total_y
        mid[:, :, cols(c)] = total_y.astype(bf16)
        for d, peer in enumerate(z_peers):
            at = pl.ds(pl.multiple_of(z_at[d] * blk, blk), blk)
            send(mid.at[:, at, cols(c)], zr.at[d, :, :, cols(c)], zs.at[c], zrs.at[c], peer)

    def sum_z(c):
        drain(zr.at[:, :, :, cols(c)], zrs.at[c])
        drain(zr.at[:, :, :, cols(c)], zs.at[c])
        both = own[lax.rem(c, keep), :, pl.ds(pl.multiple_of(z * blk, blk), blk), :]
        for d in range(nz - 1):
            both = both + zr[d, :, :, cols(c)].astype(f32)
        pre, hid = both[0], both[1]
        t = jnp.tanh(gelu_c * (pre + gelu_k * pre * pre * pre))
        slope = 0.5 * (1.0 + t) + 0.5 * pre * (1.0 - t * t) * gelu_c * (
            1.0 + 3.0 * gelu_k * pre * pre
        )
        out[0, block(z), cols(c)] = (0.5 * pre * (1.0 + t)).astype(bf16)
        out[1, block(z), cols(c)] = (hid * slope).astype(bf16)
        at = out.at[:, block(z), cols(c)]
        for peer in z_peers:
            send(at, at, azs.at[c], azr.at[c], peer)

    def give_y(c):
        drain(zr.at[:, :, :, cols(c)], azr.at[c])
        drain(zr.at[:, :, :, cols(c)], azs.at[c])
        at = out.at[:, own_half, cols(c)]
        send(at, at, ays.at[c], ayr.at[c], y_peer)

    def back(c):
        slot = lax.rem(c, 2)

        @pl.when(c + 1 < chunks)
        def _():
            for copy in fetch(c + 1, w1b, w2b, wsem_b):
                copy.start()

        for copy in fetch(c, w1b, w2b, wsem_b):
            copy.wait()
        drain(yr.at[:, :, cols(c)], ayr.at[c])
        drain(yr.at[:, :, cols(c)], ays.at[c])

        @pl.loop(0, total // rows_step)
        def _(i):
            r = pl.ds(pl.multiple_of(i * rows_step, rows_step), rows_step)
            acc[r, :feats] += jnp.dot(out[0, r, cols(c)], w2b[slot], preferred_element_type=f32)
            acc[r, feats:] += dot_last(out[1, r, cols(c)], w1b[slot])

    stages = (front, sum_y, sum_z, give_y, back)

    @pl.loop(0, chunks + LAG * (len(stages) - 1))
    def _(s):
        for n, stage in enumerate(stages):
            c = s - n * LAG

            @pl.when(jnp.logical_and(c >= 0, c < chunks))
            def _(stage=stage, c=c):
                stage(c)

    ends[...] = acc[...].astype(bf16)


def per_device(nrow, ncol, tokens, in_weight, out_weight, out_grad):
    nz = nrow // 2
    share, feats = tokens.shape
    total = share * ncol
    hid = in_weight.shape[1]
    width = 256
    chunks = hid // width
    half, blk = total // 2, total // nrow
    vmem = pl.BlockSpec(memory_space=pltpu.VMEM)
    hbm = pl.BlockSpec(memory_space=pl.ANY)
    dma = pltpu.SemaphoreType.DMA
    both, ends, all_tokens, all_grads = pl.pallas_call(
        functools.partial(kernel, nz, ncol, chunks, width),
        out_shape=(
            jax.ShapeDtypeStruct((2, total, hid), bf16),
            jax.ShapeDtypeStruct((total, 2 * feats), bf16),
            jax.ShapeDtypeStruct((total, feats), bf16),
            jax.ShapeDtypeStruct((total, feats), bf16),
        ),
        in_specs=[vmem, vmem, hbm, hbm],
        out_specs=(vmem,) * 4,
        scratch_shapes=[
            pltpu.VMEM((2, half, hid), bf16),
            pltpu.VMEM((2, half, hid), bf16),
            pltpu.VMEM((2 * LAG + 1, 2, half, width), f32),
            pltpu.VMEM((total, 2 * feats), f32),
            pltpu.VMEM((2, half, hid), bf16),
            pltpu.VMEM((nz - 1, 2, blk, hid), bf16),
            pltpu.VMEM((2, feats, width), bf16),
            pltpu.VMEM((2, width, feats), bf16),
            pltpu.VMEM((2, feats, width), bf16),
            pltpu.VMEM((2, width, feats), bf16),
            dma((2, 2)),
            dma((2, 2)),
            dma((2, 3)),
            dma((2, 3)),
        ]
        + [dma((chunks,))] * 8,
        compiler_params=pltpu.CompilerParams(
            collective_id=0, has_side_effects=True, vmem_limit_bytes=62 * 1024 * 1024
        ),
        cost_estimate=pl.CostEstimate(
            flops=8 * total * feats * hid,
            bytes_accessed=8 * feats * hid + 4 * total * hid,
            transcendentals=blk * hid,
        ),
    )(tokens, out_grad, in_weight, out_weight)
    ends = lax.psum_scatter(ends, "col", scatter_dimension=0, tiled=True)
    second_grad = dot_first(both[0], all_grads).astype(bf16)
    first_grad = dot_first(all_tokens, both[1]).astype(bf16)
    return (ends[:, :feats], ends[:, feats:], first_grad, second_grad)


def solution(mesh):
    return jax.shard_map(
        functools.partial(per_device, mesh.shape["row"], mesh.shape["col"]),
        mesh=mesh,
        in_specs=(P("col", "row"), P("row", "col"), P("col", "row"), P("col", "row")),
        out_specs=(P("col", "row"), P("col", "row"), P("row", "col"), P("col", "row")),
        check_vma=False,
    )
```

```python
import functools

import jax
import jax.numpy as jnp
from jax import lax
from jax.experimental import pallas as pl
from jax.experimental.pallas import tpu as pltpu
from jax.sharding import PartitionSpec as P

gelu_c = 0.7978845608
gelu_k = 0.044715
f32, bf16 = jnp.float32, jnp.bfloat16
LAG = 2


def dot_last(left, right):
    return lax.dot_general(left, right, (((1,), (1,)), ((), ())), preferred_element_type=f32)


def dot_first(left, right):
    return lax.dot_general(left, right, (((0,), (0,)), ((), ())), preferred_element_type=f32)


def kernel(
    nz, ncol, chunks, width,
    tok, grad, w1, w2,
    out, ends, tall, gall,
    part, mid, own, acc, yr, zr, w1a, w2a, w1b, w2b,
    wsem_a, wsem_b, gs, gr, ys, yrs, zs, zrs, azs, azr, ays, ayr,
):
    row, col = lax.axis_index("row"), lax.axis_index("col")
    z, y = row // 2, row % 2
    share, total = tok.shape[0], tall.shape[0]
    half = total // 2
    blk = half // nz
    rows_step = min(256, half)
    feats = tok.shape[1]
    keep = own.shape[0]
    group, core = col // 2, col % 2
    groups = ncol // 2

    y_peer = {"row": z * 2 + (1 - y)}
    z_at = [lax.rem(z + d, nz) for d in range(1, nz)]
    z_peers = [{"row": p * 2 + y} for p in z_at]
    c_at = [lax.rem(group + d, groups) * 2 + core for d in range(1, groups)]
    c_peers = [{"col": p} for p in c_at]
    twin = {"col": group * 2 + (1 - core)}

    def cols(c):
        return pl.ds(pl.multiple_of(c * width, width), width)

    def fetch(c, b1, b2, sem):
        slot = lax.rem(c, 2)
        return (
            pltpu.make_async_copy(w1.at[:, cols(c)], b1.at[slot], sem.at[slot, 0]),
            pltpu.make_async_copy(w2.at[cols(c), :], b2.at[slot], sem.at[slot, 1]),
        )

    for copy in fetch(0, w1a, w2a, wsem_a) + fetch(0, w1b, w2b, wsem_b):
        copy.start()

    barrier = pltpu.get_barrier_semaphore()
    peers = [y_peer, twin] + z_peers + c_peers
    for peer in peers:
        pl.semaphore_signal(barrier, inc=1, device_id=peer, device_id_type=pl.DeviceIdType.MESH)
    pl.semaphore_wait(barrier, len(peers))

    def send(src, dst, s_sem, r_sem, peer):
        pltpu.make_async_remote_copy(
            src_ref=src, dst_ref=dst, send_sem=s_sem, recv_sem=r_sem,
            device_id=peer, device_id_type=pl.DeviceIdType.MESH,
        ).start()

    def drain(like, sem):
        pltpu.make_async_copy(like, like, sem).wait()

    def place(p):
        return pl.ds(pl.multiple_of(p * share, share), share)

    gathers = ((tok, tall), (grad, gall))
    for n, (src, dst) in enumerate(gathers):
        for peer in c_peers:
            send(src, dst.at[place(col)], gs.at[n, 0], gr.at[n, 0], peer)
    for n, (src, dst) in enumerate(gathers):
        send(src, dst.at[place(col)], gs.at[n, 1], gr.at[n, 1], twin)
    tall[place(col)] = tok[...]
    gall[place(col)] = grad[...]
    acc[...] = jnp.zeros_like(acc)
    rest, one = pl.ds(0, (groups - 1) * share), pl.ds(0, share)
    for n, (src, dst) in enumerate(gathers):
        drain(dst.at[rest], gr.at[n, 0])
        for p in c_at:
            send(dst.at[place(p)], dst.at[place(p)], gs.at[n, 2], gr.at[n, 2], twin)
    for n, (src, dst) in enumerate(gathers):
        drain(dst.at[rest], gs.at[n, 0])
        drain(dst.at[one], gs.at[n, 1])
        drain(dst.at[one], gr.at[n, 1])
        drain(dst.at[rest], gs.at[n, 2])
        drain(dst.at[rest], gr.at[n, 2])

    own_half = pl.ds(pl.multiple_of(y * half, half), half)

    def block(p):
        return pl.ds(pl.multiple_of(p * blk, blk), blk)

    def is_wide(c):
        return lax.rem(c, 3) == 1

    z_right = {"row": lax.rem(z + 1, nz) * 2 + y}
    z_left = {"row": lax.rem(z + nz - 1, nz) * 2 + y}

    def hop_like(c, wide):
        return yr.at[:, pl.ds(0, 2 * blk if wide else blk), cols(c)]

    def hop_at(c, p, wide):
        return out.at[:, :, block(p), cols(c)] if wide else out.at[:, y, block(p), cols(c)]

    def hop_send(c, h, wide):
        @pl.when(jnp.logical_and(z - h >= 0, z + 1 < nz))
        def _():
            at = hop_at(c, z - h, wide)
            send(at, at, azs.at[c, 0, h], azr.at[c, 0, h], z_right)

        @pl.when(jnp.logical_and(z + h < nz, z >= 1))
        def _():
            at = hop_at(c, z + h, wide)
            send(at, at, azs.at[c, 1, h], azr.at[c, 1, h], z_left)

    def hop_wait(c, h, wide):
        like = hop_like(c, wide)

        @pl.when(z - 1 - h >= 0)
        def _():
            drain(like, azr.at[c, 0, h])

        @pl.when(z + 1 + h < nz)
        def _():
            drain(like, azr.at[c, 1, h])

        @pl.when(jnp.logical_and(z - h >= 0, z + 1 < nz))
        def _():
            drain(like, azs.at[c, 0, h])

        @pl.when(jnp.logical_and(z + h < nz, z >= 1))
        def _():
            drain(like, azs.at[c, 1, h])

    def y_send(c, wide):
        at = out.at[:, y, block(z), cols(c)] if wide else out.at[:, y, :, cols(c)]
        send(at, at, ays.at[c], ayr.at[c], y_peer)

    def y_wait(c, wide):
        like = hop_like(c, False) if wide else yr.at[:, :, cols(c)]
        drain(like, ayr.at[c])
        drain(like, ays.at[c])

    def per_mode(c, f):
        for wide in (False, True):
            @pl.when(is_wide(c) == wide)
            def _(wide=wide):
                f(wide)

    def spread(j, c):
        def f(wide):
            if wide:
                if j == 1:
                    y_wait(c, wide)
                elif j > 1:
                    hop_wait(c, j - 2, wide)
                if j == 0:
                    y_send(c, wide)
                else:
                    hop_send(c, j - 1, wide)
            else:
                if j > 0:
                    hop_wait(c, j - 1, wide)
                if j < nz - 1:
                    hop_send(c, j, wide)
                else:
                    y_send(c, wide)

        per_mode(c, f)

    def last_wait(c):
        per_mode(c, lambda wide: hop_wait(c, nz - 2, wide) if wide else y_wait(c, wide))

    def front(c):
        slot = lax.rem(c, 2)

        @pl.when(c + 1 < chunks)
        def _():
            for copy in fetch(c + 1, w1a, w2a, wsem_a):
                copy.start()

        for copy in fetch(c, w1a, w2a, wsem_a):
            copy.wait()

        def rows(base, i):
            return pl.ds(pl.multiple_of(base * half + i * rows_step, rows_step), rows_step)

        @pl.loop(0, half // rows_step)
        def _(i):
            r, to = rows(1 - y, i), rows(0, i)
            part[0, to, cols(c)] = jnp.dot(
                tall[r, :], w1a[slot], preferred_element_type=f32
            ).astype(bf16)
            part[1, to, cols(c)] = dot_last(gall[r, :], w2a[slot]).astype(bf16)

        at = yr.at[:, :, cols(c)]
        send(part.at[:, :, cols(c)], at, ys.at[c], yrs.at[c], y_peer)
        mine = lax.rem(c, keep)

        @pl.loop(0, half // rows_step)
        def _(i):
            r, to = rows(y, i), rows(0, i)
            own[mine, 0, to, :] = jnp.dot(tall[r, :], w1a[slot], preferred_element_type=f32)
            own[mine, 1, to, :] = dot_last(gall[r, :], w2a[slot])

    def sum_y(c):
        drain(yr.at[:, :, cols(c)], yrs.at[c])
        drain(yr.at[:, :, cols(c)], ys.at[c])
        mine = lax.rem(c, keep)
        total_y = own[mine] + yr[:, :, cols(c)].astype(f32)
        own[mine] = total_y
        mid[:, :, cols(c)] = total_y.astype(bf16)
        for d, peer in enumerate(z_peers):
            at = pl.ds(pl.multiple_of(z_at[d] * blk, blk), blk)
            send(mid.at[:, at, cols(c)], zr.at[d, :, :, cols(c)], zs.at[c], zrs.at[c], peer)

    def sum_z(c):
        drain(zr.at[:, :, :, cols(c)], zrs.at[c])
        drain(zr.at[:, :, :, cols(c)], zs.at[c])
        both = own[lax.rem(c, keep), :, pl.ds(pl.multiple_of(z * blk, blk), blk), :]
        for d in range(nz - 1):
            both = both + zr[d, :, :, cols(c)].astype(f32)
        pre, hid = both[0], both[1]
        t = jnp.tanh(gelu_c * (pre + gelu_k * pre * pre * pre))
        slope = 0.5 * (1.0 + t) + 0.5 * pre * (1.0 - t * t) * gelu_c * (
            1.0 + 3.0 * gelu_k * pre * pre
        )
        out[0, y, block(z), cols(c)] = (0.5 * pre * (1.0 + t)).astype(bf16)
        out[1, y, block(z), cols(c)] = (hid * slope).astype(bf16)
        spread(0, c)

    def back(c):
        slot = lax.rem(c, 2)

        @pl.when(c + 1 < chunks)
        def _():
            for copy in fetch(c + 1, w1b, w2b, wsem_b):
                copy.start()

        for copy in fetch(c, w1b, w2b, wsem_b):
            copy.wait()
        last_wait(c)

        @pl.loop(0, total // rows_step)
        def _(i):
            r = pl.ds(pl.multiple_of(i * rows_step, rows_step), rows_step)
            side = i // (half // rows_step)
            at = pl.ds(pl.multiple_of(i * rows_step - side * half, rows_step), rows_step)
            acc[r, :feats] += jnp.dot(out[0, side, at, cols(c)], w2b[slot], preferred_element_type=f32)
            acc[r, feats:] += dot_last(out[1, side, at, cols(c)], w1b[slot])

    spreads = tuple(functools.partial(spread, j) for j in range(1, nz))
    stages = (front, sum_y, sum_z) + spreads + (back,)

    @pl.loop(0, chunks + LAG * (len(stages) - 1))
    def _(s):
        for n, stage in enumerate(stages):
            c = s - n * LAG

            @pl.when(jnp.logical_and(c >= 0, c < chunks))
            def _(stage=stage, c=c):
                stage(c)

    ends[...] = acc[...].astype(bf16)


def per_device(nrow, ncol, tokens, in_weight, out_weight, out_grad):
    nz = nrow // 2
    share, feats = tokens.shape
    total = share * ncol
    hid = in_weight.shape[1]
    width = 256
    chunks = hid // width
    half, blk = total // 2, total // nrow
    vmem = pl.BlockSpec(memory_space=pltpu.VMEM)
    hbm = pl.BlockSpec(memory_space=pl.ANY)
    dma = pltpu.SemaphoreType.DMA
    both, ends, all_tokens, all_grads = pl.pallas_call(
        functools.partial(kernel, nz, ncol, chunks, width),
        out_shape=(
            jax.ShapeDtypeStruct((2, 2, half, hid), bf16),
            jax.ShapeDtypeStruct((total, 2 * feats), bf16),
            jax.ShapeDtypeStruct((total, feats), bf16),
            jax.ShapeDtypeStruct((total, feats), bf16),
        ),
        in_specs=[vmem, vmem, hbm, hbm],
        out_specs=(vmem,) * 4,
        scratch_shapes=[
            pltpu.VMEM((2, half, hid), bf16),
            pltpu.VMEM((2, half, hid), bf16),
            pltpu.VMEM((2 * LAG + 1, 2, half, width), f32),
            pltpu.VMEM((total, 2 * feats), f32),
            pltpu.VMEM((2, half, hid), bf16),
            pltpu.VMEM((nz - 1, 2, blk, hid), bf16),
            pltpu.VMEM((2, feats, width), bf16),
            pltpu.VMEM((2, width, feats), bf16),
            pltpu.VMEM((2, feats, width), bf16),
            pltpu.VMEM((2, width, feats), bf16),
            dma((2, 2)),
            dma((2, 2)),
            dma((2, 3)),
            dma((2, 3)),
        ]
        + [dma((chunks,))] * 4
        + [dma((chunks, 2, nz - 1))] * 2
        + [dma((chunks,))] * 2,
        compiler_params=pltpu.CompilerParams(
            collective_id=0, has_side_effects=True, vmem_limit_bytes=62 * 1024 * 1024
        ),
        cost_estimate=pl.CostEstimate(
            flops=8 * total * feats * hid,
            bytes_accessed=8 * feats * hid + 4 * total * hid,
            transcendentals=blk * hid,
        ),
    )(tokens, out_grad, in_weight, out_weight)
    both = both.reshape(2, total, hid)
    ends = lax.psum_scatter(ends, "col", scatter_dimension=0, tiled=True)
    second_grad = dot_first(both[0], all_grads).astype(bf16)
    first_grad = dot_first(all_tokens, both[1]).astype(bf16)
    return (ends[:, :feats], ends[:, feats:], first_grad, second_grad)


def solution(mesh):
    return jax.shard_map(
        functools.partial(per_device, mesh.shape["row"], mesh.shape["col"]),
        mesh=mesh,
        in_specs=(P("col", "row"), P("row", "col"), P("col", "row"), P("col", "row")),
        out_specs=(P("col", "row"), P("col", "row"), P("row", "col"), P("col", "row")),
        check_vma=False,
    )
```
